32 devices in a mesh: dom: 8 (over z, y), sub: 4 (over x, core).
Axes of the slice: x: 2, y: 2, z: 4, core: 2. Of those that a mesh axis runs over, the one named last changes fastest.
Arguments:
- pair_blocks: bfloat16 [2048, 128, 128], P(('dom', 'sub')), may hold values from -0.5 to 0.5
- pair_centers: bfloat16 [2048, 2, 3, 128], P(('dom', 'sub')), may hold values from 0 to 8
- pair_expo: bfloat16 [2048, 2, 128], P(('dom', 'sub')), may hold values from 0.049804688 to 0.5
- pair_linear_terms: bfloat16 [2048, 2, 3, 128], P(('dom', 'sub')), may hold values from -0.14941406 to 0.14941406
- pair_dest: int32 [2048, 1], P(('dom', 'sub')), may hold values from 0 to 7; in each aligned block of 64 rows (0 to 63, 64 to 127, ...) at most 16 rows name the same one
- pair_tiles: int32 [2048, 2], P(('dom', 'sub')), may hold values from 0 to 31
- slab_from: int32 [32, 8], P(('dom', 'sub')), may hold values from 0 to 7, each once within a row
Outputs:
- wave_slab_density: float32 [256, 512], P(('dom', 'sub'))
The draws below stay inside these ranges and needn't reach their ends.
Inputs may be any that keep to these rules, and one draw needn't show every extreme that they name: `pair_dest`: in the rows of one device no domain is named by more than 16 rows. `slab_from`: each row is a permutation.
All inputs are finite; a program needn't handle non-finite values.
Results may differ from the reference program's by a relative error of at most 0.0028.
Values may be sent and summed in bfloat16 or wider, within the bound.
No kernel may reach another device: no remote copies, remote signals or barrier semaphores. Data moves between devices by JAX's collectives and lax.ppermute only.
A program may use at most 64 MiB of HBM per device.

```python
import math
import jax
import jax.numpy as jnp
import numpy as np
from jax import lax

FB = 128
TE = 8
TPB = 2
TPD = 4
NB_DEV = 64
CAPB = 16
LT = 32
QS = 1
ROWS_DEV = 8
BLOCKS = 2048
N_DOM = 8
N_SUB = 4
DEVICES = 32


def set_ends(values, key, least, top_value):
    extent = values.shape
    place = [jax.random.randint(jax.random.fold_in(key, axis), (), 0, extent[axis]) for axis in range(len(extent))]
    values = values.at[tuple(place)].set(least)
    longest = extent.index(max(extent))
    place[longest] = (place[longest] + 1) % extent[longest]
    return values.at[tuple(place)].set(top_value)


def block_scale(rng, shape, shards, smallest, top_value):
    factor_of, own = 1.0, jax.random.fold_in(rng, 6)
    for position, blocks in shards:
        steps = jnp.exp(jax.random.uniform(jax.random.fold_in(own, position), (blocks,), jnp.float32, smallest / len(shards), top_value / len(shards)))
        factor_of = factor_of * jnp.repeat(steps, shape[position] // blocks).reshape([-1 if axis == position else 1 for axis in range(len(shape))])
    return factor_of


def deal_out(key, own, number, rows, amount, top, limit, skew):
    ranking = jax.random.permutation(key, amount)
    heavy_load, common = portions_of(amount, rows * top, limit, skew, True), portions_of(amount, rows * top, limit, skew, False)
    places = jnp.arange(amount)

    def named(tallies, rotation):
        used = int((tallies > 0).sum())
        fixed = max(1, used // 4)
        moved = fixed + (places - fixed + rotation * (used - fixed)) % max(1, amount - fixed)
        return jnp.zeros((amount,), jnp.int32).at[ranking[jnp.where(places < fixed, places, moved)]].set(jnp.asarray(tallies, jnp.int32))

    tallies = jnp.where(number % 4 == 0, named(heavy_load, number // 4), named(common, number - number // 4 - 1))
    mixed = jax.random.permutation(jax.random.fold_in(own, 3), amount)
    giver, taker = mixed[0:amount // 2 * 2:2], mixed[1:amount // 2 * 2:2]
    slack = jnp.minimum(tallies[giver] - 1, limit - tallies[taker]) // 2
    slack = jnp.where((giver == ranking[0]) | (taker == ranking[0]) | (tallies[taker] == 0), 0, jnp.maximum(slack, 0))
    moved = jax.random.randint(jax.random.fold_in(own, 4), (amount // 2,), 0, 1 << 20) % (slack + 1)
    tallies = tallies.at[giver].add(-moved).at[taker].add(moved)
    items = jnp.searchsorted(jnp.cumsum(tallies), jnp.arange(rows * top), side="right").astype(jnp.int32)
    grid = items.reshape(top, rows).T
    grid = grid[jax.random.permutation(jax.random.fold_in(own, 1), rows)]
    rotation = jax.random.randint(jax.random.fold_in(own, 2), (rows, 1), 0, top)
    return jnp.take_along_axis(grid, (jnp.arange(top)[None, :] + rotation) % top, axis=1)


def portions_of(number_of, total, bound, lean, full):
    loads = [(1 << 20) // math.isqrt(grade ** lean) + 1 for grade in range(1, number_of + 1)]
    largest = bound if full else min(bound, max(-(-total // number_of), total * loads[0] // sum(loads)))
    least = 1 if total - largest >= number_of - 1 else 0
    counts, surplus = [largest] + [least] * (number_of - 1), total - largest - least * (number_of - 1)
    while surplus > 0:
        free = [i for i in range(1, number_of) if counts[i] < largest] or [i for i in range(1, number_of) if counts[i] < bound]
        mass, budget = sum([loads[i] for i in free]), surplus
        for i in free:
            more = min(bound - counts[i], max(1, budget * loads[i] // mass), surplus)
            counts[i] = counts[i] + more
            surplus = surplus - more
    return np.array(counts)


def centred(rng, extent, width, reach, cuts=(), kind=jnp.bfloat16):
    gain = block_scale(rng, extent, cuts, -0.22, 0.18) if cuts else 1.0
    entries = jax.random.normal(rng, extent, jnp.float32) * width * gain
    return jnp.minimum(jnp.maximum(entries, -reach), reach).astype(kind)


def setup_inputs(seed: int = 0) -> dict:
    arg_keys = jax.random.split(jax.random.key(seed), 8)
    pair_blocks = centred(arg_keys[0], (BLOCKS, FB, FB), FB ** -0.5, 0.5, ((0, 32),))
    pair_centers = jnp.clip(8.0 * jax.random.uniform(arg_keys[1], (BLOCKS, 2, 3, FB), jnp.float32) ** block_scale(arg_keys[1], (BLOCKS, 2, 3, FB), ((0, 32),), -0.2, 0.2), 0.0, 8.0).astype(jnp.bfloat16)
    pair_expo = jnp.clip(jnp.exp(math.log(0.5) - 2.306499 * jax.random.uniform(arg_keys[2], (BLOCKS, 2, FB), jnp.float32) ** block_scale(arg_keys[2], (BLOCKS, 2, FB), ((0, 32),), -0.2, 0.2)), 0.049804688, 0.5).astype(jnp.bfloat16)
    pair_linear_terms = jnp.clip(jax.random.uniform(arg_keys[3], (BLOCKS, 2, 3, FB), jnp.float32, -0.14941406, 0.14941406) * block_scale(arg_keys[3], (BLOCKS, 2, 3, FB), ((0, 32),), -0.4, 0.0), -0.14941406, 0.14941406).astype(jnp.bfloat16)
    pair_dest_keys = jax.random.split(jax.random.fold_in(arg_keys[4], 1), BLOCKS // NB_DEV)
    pair_dest_turns = jax.random.permutation(jax.random.fold_in(arg_keys[4], 3), BLOCKS // NB_DEV)
    pair_dest = jax.vmap(lambda own, number: deal_out(jax.random.fold_in(arg_keys[4], 2), own, number, NB_DEV, N_DOM, 1, CAPB, 2))(pair_dest_keys, pair_dest_turns).reshape((BLOCKS, 1))
    pair_tiles = set_ends(jax.random.randint(arg_keys[5], (BLOCKS, TPB), 0, LT), jax.random.fold_in(arg_keys[5], 1), 0, LT - 1).astype(jnp.int32)
    slab_from = jax.vmap(lambda own: jax.random.permutation(own, ROWS_DEV))(jax.random.split(arg_keys[6], DEVICES)).reshape((DEVICES, ROWS_DEV)).astype(jnp.int32)
    return {"pair_blocks": pair_blocks, "pair_centers": pair_centers, "pair_expo": pair_expo, "pair_linear_terms": pair_linear_terms, "pair_dest": pair_dest, "pair_tiles": pair_tiles, "slab_from": slab_from}


def region_points():
    tile_cells = TE ** 3
    index = jnp.arange(TPB * tile_cells, dtype=jnp.int32)
    coord_x = (index // tile_cells) * TE + (index % tile_cells) // (TE * TE)
    coord_y = (index // TE) % TE
    coord_z = index % TE
    return [coord_x.astype(jnp.float32), coord_y.astype(jnp.float32), coord_z.astype(jnp.float32)]


def basis_values(centers, expo, slope):
    points = region_points()
    stretch = [float(TPB), 1.0, 1.0]
    radius = jnp.zeros((), jnp.float32)
    linear = jnp.ones((), jnp.float32)
    for axis_index in range(3):
        middle_point = stretch[axis_index] * centers[:, :, axis_index, :].astype(jnp.float32)
        offset = points[axis_index][None, None, None, :] - middle_point[..., None]
        radius = radius + offset * offset
        linear = linear + slope[:, :, axis_index, :].astype(jnp.float32)[..., None] * offset
    return linear * jnp.exp(-expo.astype(jnp.float32)[..., None] * radius)


def group_density(block_list, centers, expo, slope):
    values = basis_values(centers, expo, slope)
    right_factor = lax.optimization_barrier(values[:, 1].astype(jnp.bfloat16))
    pair_product = jnp.einsum("pck,pka->pca", block_list.astype(jnp.float32), right_factor.astype(jnp.float32))
    density = 2.0 * jnp.sum(values[:, 0] * pair_product, axis=1)
    return density.reshape(block_list.shape[0], TPB, TE ** 3)


def reference(pair_blocks, pair_centers, pair_expo, pair_linear_terms, pair_dest, pair_tiles, slab_from):
    group_size = 16
    group_count = pair_blocks.shape[0] // group_size

    def handle(items):
        return group_density(items[0], items[1], items[2], items[3])

    density_all = lax.map(handle, (pair_blocks.reshape(group_count, group_size, FB, FB), pair_centers.reshape(group_count, group_size, 2, 3, FB), pair_expo.reshape(group_count, group_size, 2, FB), pair_linear_terms.reshape(group_count, group_size, 2, 3, FB)))
    density_all = density_all.reshape(-1, TE ** 3)
    tile_rows = (pair_dest[:, 0:1] * LT + pair_tiles).reshape(-1).astype(jnp.int32)
    domain_tiles = jnp.zeros((N_DOM * LT, TE ** 3), jnp.float32).at[tile_rows].add(density_all)
    device = jnp.arange(N_DOM * N_SUB, dtype=jnp.int32)
    source_dom = slab_from // QS
    within = slab_from % QS
    tile_index = source_dom * LT + (device // N_SUB)[:, None] * TPD + (device % N_SUB)[:, None] * QS + within
    return domain_tiles[tile_index.reshape(-1).astype(jnp.int32)]
```

```python
import functools

import jax
import jax.numpy as jnp
from jax import lax
from jax.experimental import pallas as pl
from jax.experimental.pallas import tpu as pltpu
from jax.sharding import PartitionSpec as P

TE = 8
TPB = 2
TPD = 4
CELLS = TE**3
PLANE = TE * TE
AXES = ("dom", "sub")
STEP_BLOCKS = 8
DENSE_ROWS = 1024


def side_factors(center, expo, slope):
    width = expo.shape[-1]

    def steps(count):
        return lax.broadcasted_iota(jnp.int32, (count, width), 0).astype(jnp.float32)

    ux = steps(TPB * TE) - float(TPB) * center[0]
    uy = steps(TE) - center[1]
    uz = steps(TE) - center[2]
    ex = jnp.exp(-expo * (ux * ux))
    ey = jnp.exp(-expo * (uy * uy))
    ez = jnp.exp(-expo * (uz * uz))
    yz = ey[:, None, :] * ez[None]
    head = (1.0 - slope[0] * (float(TPB) * center[0])) + slope[1] * uy
    t = yz * (head[:, None, :] + (slope[2] * uz)[None])
    d = yz * slope[0][None]
    return ex, t, d


def density_kernel(
    blocks_ref, center_ref, expo_ref, slope_ref, row_ref, out_ref, weight, column, scaled, spread, total
):
    step = pl.program_id(0)
    count, width = blocks_ref.shape[0], blocks_ref.shape[1]
    row_count = out_ref.shape[0]

    @pl.when(step == 0)
    def _():
        weight[...] = jnp.zeros_like(weight)
        total[...] = jnp.zeros_like(total)

    def factors(i, which):
        center = center_ref[i].astype(jnp.float32)
        expo = expo_ref[i].astype(jnp.float32)
        slope = slope_ref[i].astype(jnp.float32)
        return side_factors(
            [center[which, a : a + 1] for a in range(3)],
            expo[which : which + 1],
            [slope[which, a : a + 1] for a in range(3)],
        )

    rows = row_ref[...]
    lanes = lax.broadcasted_iota(jnp.int32, (count, row_count), 1)
    hot = [jnp.where(rows[:, k : k + 1] == lanes, 2.0, 0.0) for k in range(TPB)]
    for pair in range(count // 2):
        for h in range(2):
            i = 2 * pair + h
            own = slice(h * width, (h + 1) * width)
            weight[pair, own, own] = blocks_ref[i]
            ex, t, d = factors(i, 1)
            for x in range(TPB * TE):
                value = (t * ex[x : x + 1][None]).reshape(PLANE, width)
                column[pair, x * PLANE : (x + 1) * PLANE, own] = value.astype(jnp.bfloat16)
                t = t + d
            for k in range(TPB):
                slot = (TPB * i + k) * width
                spread[slot : slot + width, :] = jnp.broadcast_to(
                    hot[k][i : i + 1], (width, row_count)
                ).astype(jnp.bfloat16)
        product = lax.dot_general(
            column[pair], weight[pair], (((1,), (1,)), ((), ())), preferred_element_type=jnp.float32
        )
        for h in range(2):
            i = 2 * pair + h
            ex, t, d = factors(i, 0)
            for x in range(TPB * TE):
                part = product[x * PLANE : (x + 1) * PLANE, h * width : (h + 1) * width]
                value = (t * ex[x : x + 1][None]).reshape(PLANE, width) * part
                k, q = x // TE, x % TE
                slot = (TPB * i + k) * width
                scaled[q * PLANE : (q + 1) * PLANE, slot : slot + width] = value.astype(jnp.bfloat16)
                t = t + d
    total[...] += jnp.dot(scaled[...], spread[...], preferred_element_type=jnp.float32)

    @pl.when(step == pl.num_programs(0) - 1)
    def _():
        out_ref[...] = total[...].T.astype(out_ref.dtype)


def tile_sums(blocks, center, expo, slope, rows, row_count, out_type):
    number, width = blocks.shape[0], blocks.shape[1]
    per_step = STEP_BLOCKS

    def split(*rest):
        return pl.BlockSpec((per_step,) + rest, lambda g: (g,) + (0,) * len(rest))

    return pl.pallas_call(
        density_kernel,
        grid=(number // per_step,),
        in_specs=[
            split(width, width),
            split(2, 3, width),
            split(2, width),
            split(2, 3, width),
            split(TPB),
        ],
        out_specs=pl.BlockSpec((row_count, CELLS), lambda g: (0, 0)),
        out_shape=jax.ShapeDtypeStruct((row_count, CELLS), out_type),
        scratch_shapes=[
            pltpu.VMEM((per_step // 2, 2 * width, 2 * width), jnp.bfloat16),
            pltpu.VMEM((per_step // 2, TPB * CELLS, 2 * width), jnp.bfloat16),
            pltpu.VMEM((CELLS, per_step * TPB * width), jnp.bfloat16),
            pltpu.VMEM((per_step * TPB * width, row_count), jnp.bfloat16),
            pltpu.VMEM((CELLS, row_count), jnp.float32),
        ],
        compiler_params=pltpu.CompilerParams(vmem_limit_bytes=48 << 20),
    )(blocks, center, expo, slope, rows)


def pick_rows(summed, order):
    match = order[:, None] == jnp.arange(summed.shape[0], dtype=jnp.int32)[None, :]
    return jnp.sum(jnp.where(match[:, :, None], summed[None], 0.0), axis=1)


def dense_plan(blocks, center, expo, slope, dest, tiles, order, dom_count, sub_count):
    quarter = TPD // sub_count
    held = dom_count * quarter
    rows = tiles // quarter * held + dest * quarter + tiles % quarter
    partial = tile_sums(
        blocks, center, expo, slope, rows, dom_count * sub_count * held, jnp.bfloat16
    )
    moved = lax.all_to_all(
        partial.reshape(dom_count * sub_count, held, CELLS), AXES, split_axis=0, concat_axis=0, tiled=True
    )
    return pick_rows(jnp.sum(moved.astype(jnp.float32), axis=0), order)


def routed_plan(blocks, center, expo, slope, dest, tiles, order, dom_count, sub_count):
    number = blocks.shape[0]
    capacity = max(2, 2 * number // dom_count)
    tile_count = dom_count * TPD
    quarter = TPD // sub_count
    own_rows = jnp.arange(TPB * number, dtype=jnp.int32).reshape(number, TPB)
    density = tile_sums(blocks, center, expo, slope, own_rows, TPB * number, jnp.float32)
    density = density.reshape(number, TPB, CELLS).astype(jnp.bfloat16)
    targets = dest[:, 0]
    one_hot = (targets[:, None] == jnp.arange(dom_count, dtype=jnp.int32)[None, :]).astype(jnp.int32)
    places = jnp.sum((jnp.cumsum(one_hot, axis=0) - one_hot) * one_hot, axis=1)

    def exchange(values, filler):
        holder = jnp.full((dom_count, capacity) + values.shape[1:], filler, values.dtype)
        holder = holder.at[targets, places].set(values)
        return lax.all_to_all(holder, "dom", split_axis=0, concat_axis=0, tiled=True)

    arrived = exchange(density, 0).reshape(-1, CELLS).astype(jnp.float32)
    tile_ids = exchange(tiles, tile_count).reshape(-1)
    partial = jnp.zeros((tile_count, CELLS), jnp.float32).at[tile_ids].add(arrived, mode="drop")
    moved = lax.all_to_all(
        partial.reshape(dom_count, TPD, CELLS), "dom", split_axis=0, concat_axis=0, tiled=True
    )
    summed = lax.psum_scatter(moved, "sub", scatter_dimension=1, tiled=True)
    return summed.reshape(dom_count * quarter, CELLS)[order]


def local(blocks, center, expo, slope, dest, tiles, slab_from):
    dom_count, sub_count = lax.axis_size("dom"), lax.axis_size("sub")
    all_rows = dom_count * dom_count * TPD
    plan = dense_plan if all_rows <= DENSE_ROWS else routed_plan
    return plan(blocks, center, expo, slope, dest, tiles, slab_from[0], dom_count, sub_count)


def solution(mesh):
    def placed(rank):
        return P(AXES, *([None] * (rank - 1)))

    return jax.shard_map(
        local,
        mesh=mesh,
        in_specs=tuple(placed(rank) for rank in (3, 4, 3, 4, 2, 2, 2)),
        out_specs=placed(2),
        check_vma=False,
    )
```

```python
import functools

import jax
import jax.numpy as jnp
from jax import lax
from jax.experimental import pallas as pl
from jax.experimental.pallas import tpu as pltpu
from jax.sharding import PartitionSpec as P

TE = 8
TPB = 2
TPD = 4
CELLS = TE**3
PLANE = TE * TE
AXES = ("dom", "sub")
STEP_BLOCKS = 16
LOG2_E = 1.4426950408889634
DENSE_ROWS = 1024


def side_factors(center, expo, slope, table):
    width = expo.shape[-1]
    steps = lax.broadcasted_iota(jnp.int32, (TE, width), 0).astype(jnp.float32)
    center_x = float(TPB) * center[0]
    rate = expo * (-LOG2_E)
    uy = steps - center[1]
    uz = steps - center[2]
    for k in range(TPB):
        ux = (steps + float(k * TE)) - center_x
        table[k * TE : (k + 1) * TE, :] = jnp.exp2(rate * (ux * ux))
    y_rows, slope_rows = TPB * TE, (TPB + 1) * TE
    table[y_rows : y_rows + TE, :] = jnp.exp2(rate * (uy * uy))
    table[slope_rows : slope_rows + TE, :] = (1.0 - slope[0] * center_x) + slope[1] * uy
    ez = jnp.exp2(rate * (uz * uz))
    z_part = slope[2] * uz

    def row(index):
        return jnp.broadcast_to(table[index : index + 1, :], (TE, width))

    yz = [row(y_rows + y) * ez for y in range(TE)]
    t = jnp.stack([yz[y] * (row(slope_rows + y) + z_part) for y in range(TE)])
    d = jnp.stack([value * slope[0] for value in yz])
    return row, t, d


def density_kernel(
    dest_ref,
    tile_ref,
    blocks_ref,
    center_ref,
    expo_ref,
    slope_ref,
    out_ref,
    weight,
    total,
    centers,
    expos,
    slopes,
    tables,
    *columns,
    row_of,
):
    step = pl.program_id(0)
    count, width = blocks_ref.shape[0], blocks_ref.shape[1]
    cell_rows = 4 * PLANE

    @pl.when(step == 0)
    def _():
        weight[...] = jnp.zeros_like(weight)
        total[...] = jnp.zeros_like(total)
        centers[...] = center_ref[...].astype(jnp.float32)
        expos[...] = expo_ref[...].astype(jnp.float32)
        slopes[...] = slope_ref[...].astype(jnp.float32)

    def factors(block, which, slot):
        def spread(ref, index):
            return jnp.broadcast_to(ref[pl.ds(index, 1), :], (TE, width))

        return side_factors(
            [spread(centers, 6 * block + 2 * a + which) for a in range(3)],
            spread(expos, 2 * block + which),
            [spread(slopes, 6 * block + 2 * a + which) for a in range(3)],
            tables.at[slot],
        )

    pick = lax.broadcasted_iota(jnp.int32, (16, 2 * width), 1) // width
    pick = (pick == lax.broadcasted_iota(jnp.int32, (16, 2 * width), 0)).astype(jnp.float32)
    pick = pick.astype(jnp.bfloat16)
    transposed = (((1,), (1,)), ((), ()))
    half_points = TPB * CELLS // 2

    for pair in range(count // 2):
        column = columns[pair]
        first = step * count + 2 * pair
        for h in range(2):
            own = slice(h * width, (h + 1) * width)
            weight[pair, own, own] = blocks_ref[2 * pair + h]
            row, t, d = factors(first + h, 1, 4 * pair + h)
            for x in range(TPB * TE):
                value = (t * row(x)[None]).reshape(PLANE, width)
                column[x * PLANE : (x + 1) * PLANE, own] = value.astype(jnp.bfloat16)
                t = t + d
        sides = [list(factors(first + h, 0, 4 * pair + 2 + h)) for h in range(2)]
        for half in range(2):
            product = lax.dot_general(
                column[half * half_points : (half + 1) * half_points, :],
                weight[pair],
                transposed,
                preferred_element_type=jnp.float32,
            )
            for part in range(half_points // cell_rows):
                scaled = []
                for h in range(2):
                    row, t, d = sides[h]
                    planes = []
                    for plane in range(4):
                        at = part * cell_rows + plane * PLANE
                        x = half * (half_points // PLANE) + part * 4 + plane
                        value = (t * row(x)[None]).reshape(PLANE, width)
                        value = value * product[at : at + PLANE, h * width : (h + 1) * width]
                        planes.append(value.astype(jnp.bfloat16))
                        t = t + d
                    sides[h][1] = t
                    scaled.append(jnp.concatenate(planes, axis=0))
                sums = lax.dot_general(
                    pick,
                    jnp.concatenate(scaled, axis=1),
                    transposed,
                    preferred_element_type=jnp.float32,
                )
                start = half * half_points + part * cell_rows
                k, q = start // CELLS, start % CELLS
                for h in range(2):
                    where = row_of(dest_ref, tile_ref, first + h, k)
                    total[pl.ds(where, 1), q : q + cell_rows] += sums[h : h + 1]

    @pl.when(step == pl.num_programs(0) - 1)
    def _():
        out_ref[...] = (2.0 * total[...]).astype(out_ref.dtype)


def tile_sums(blocks, center, expo, slope, dest, tiles, row_of, row_count, out_type):
    number, width = blocks.shape[0], blocks.shape[1]
    per_step = min(STEP_BLOCKS, number)

    def flat(values):
        return values.reshape(-1, width)

    def whole(values):
        return pl.BlockSpec(values.shape, lambda g: (0, 0))

    tables = (flat(jnp.swapaxes(center, 1, 2)), flat(expo), flat(jnp.swapaxes(slope, 1, 2)))
    scalars = pl.BlockSpec(memory_space=pltpu.SMEM)
    return pl.pallas_call(
        functools.partial(density_kernel, row_of=row_of),
        grid=(number // per_step,),
        in_specs=[
            scalars,
            scalars,
            pl.BlockSpec((per_step, width, width), lambda g: (g, 0, 0)),
            *[whole(values) for values in tables],
        ],
        out_specs=pl.BlockSpec((row_count, CELLS), lambda g: (0, 0)),
        out_shape=jax.ShapeDtypeStruct((row_count, CELLS), out_type),
        scratch_shapes=[
            pltpu.VMEM((per_step // 2, 2 * width, 2 * width), jnp.bfloat16),
            pltpu.VMEM((row_count, CELLS), jnp.float32),
            *[pltpu.VMEM(values.shape, jnp.float32) for values in tables],
            pltpu.VMEM((2 * per_step, (TPB + 2) * TE, width), jnp.float32),
            *[pltpu.VMEM((TPB * CELLS, 2 * width), jnp.bfloat16)] * (per_step // 2),
        ],
        compiler_params=pltpu.CompilerParams(vmem_limit_bytes=60 << 20),
    )(dest.T, tiles.T, blocks, *tables)


def pick_rows(summed, order):
    match = order[:, None] == jnp.arange(summed.shape[0], dtype=jnp.int32)[None, :]
    return jnp.sum(jnp.where(match[:, :, None], summed[None], 0.0), axis=1)


def dense_plan(blocks, center, expo, slope, dest, tiles, order, dom_count, sub_count):
    quarter = TPD // sub_count
    held = dom_count * quarter

    def row_of(dest_ref, tile_ref, block, k):
        tile = tile_ref[k, block]
        return tile // quarter * held + dest_ref[0, block] * quarter + tile % quarter

    partial = tile_sums(
        blocks, center, expo, slope, dest, tiles, row_of, dom_count * sub_count * held, jnp.bfloat16
    )
    moved = lax.all_to_all(
        partial.reshape(dom_count * sub_count, held, CELLS), AXES, split_axis=0, concat_axis=0, tiled=True
    )
    return pick_rows(jnp.sum(moved.astype(jnp.float32), axis=0), order)


def routed_plan(blocks, center, expo, slope, dest, tiles, order, dom_count, sub_count):
    number = blocks.shape[0]
    capacity = max(2, 2 * number // dom_count)
    tile_count = dom_count * TPD
    quarter = TPD // sub_count

    def row_of(dest_ref, tile_ref, block, k):
        return TPB * block + k

    density = tile_sums(
        blocks, center, expo, slope, dest, tiles, row_of, TPB * number, jnp.float32
    )
    density = density.reshape(number, TPB, CELLS).astype(jnp.bfloat16)
    targets = dest[:, 0]
    one_hot = (targets[:, None] == jnp.arange(dom_count, dtype=jnp.int32)[None, :]).astype(jnp.int32)
    places = jnp.sum((jnp.cumsum(one_hot, axis=0) - one_hot) * one_hot, axis=1)

    def exchange(values, filler):
        holder = jnp.full((dom_count, capacity) + values.shape[1:], filler, values.dtype)
        holder = holder.at[targets, places].set(values)
        return lax.all_to_all(holder, "dom", split_axis=0, concat_axis=0, tiled=True)

    arrived = exchange(density, 0).reshape(-1, CELLS).astype(jnp.float32)
    tile_ids = exchange(tiles, tile_count).reshape(-1)
    partial = jnp.zeros((tile_count, CELLS), jnp.float32).at[tile_ids].add(arrived, mode="drop")
    moved = lax.all_to_all(
        partial.reshape(dom_count, TPD, CELLS), "dom", split_axis=0, concat_axis=0, tiled=True
    )
    summed = lax.psum_scatter(moved, "sub", scatter_dimension=1, tiled=True)
    return summed.reshape(dom_count * quarter, CELLS)[order]


def local(blocks, center, expo, slope, dest, tiles, slab_from):
    dom_count, sub_count = lax.axis_size("dom"), lax.axis_size("sub")
    all_rows = dom_count * dom_count * TPD
    plan = dense_plan if all_rows <= DENSE_ROWS else routed_plan
    return plan(blocks, center, expo, slope, dest, tiles, slab_from[0], dom_count, sub_count)


def solution(mesh):
    def placed(rank):
        return P(AXES, *([None] * (rank - 1)))

    return jax.shard_map(
        local,
        mesh=mesh,
        in_specs=tuple(placed(rank) for rank in (3, 4, 3, 4, 2, 2, 2)),
        out_specs=placed(2),
        check_vma=False,
    )
```

```python
import functools

import jax
import jax.numpy as jnp
from jax import lax
from jax.experimental import pallas as pl
from jax.experimental.pallas import tpu as pltpu
from jax.sharding import PartitionSpec as P

TE = 8
TPB = 2
TPD = 4
CELLS = TE**3
PLANE = TE * TE
AXES = ("dom", "sub")
STEP_BLOCKS = 32
LOG2_E = 1.4426950408889634
DENSE_ROWS = 1024


def side_factors(center, expo, slope, table):
    width = expo.shape[-1]
    steps = lax.broadcasted_iota(jnp.int32, (TE, width), 0).astype(jnp.float32)
    center_x = float(TPB) * center[0]
    rate = expo * (-LOG2_E)
    uy = steps - center[1]
    uz = steps - center[2]
    for k in range(TPB):
        ux = (steps + float(k * TE)) - center_x
        table[k * TE : (k + 1) * TE, :] = jnp.exp2(rate * (ux * ux))
    y_rows, slope_rows = TPB * TE, (TPB + 1) * TE
    table[y_rows : y_rows + TE, :] = jnp.exp2(rate * (uy * uy))
    table[slope_rows : slope_rows + TE, :] = (1.0 - slope[0] * center_x) + slope[1] * uy
    ez = jnp.exp2(rate * (uz * uz))
    z_part = slope[2] * uz

    def row(index):
        return jnp.broadcast_to(table[index : index + 1, :], (TE, width))

    yz = [row(y_rows + y) * ez for y in range(TE)]
    t = jnp.stack([yz[y] * (row(slope_rows + y) + z_part) for y in range(TE)])
    d = jnp.stack([value * slope[0] for value in yz])
    return row, t, d


def density_kernel(
    dest_ref,
    tile_ref,
    blocks_ref,
    center_ref,
    expo_ref,
    slope_ref,
    out_ref,
    total,
    centers,
    expos,
    slopes,
    tables,
    *columns,
    row_of,
):
    step = pl.program_id(0)
    count, width = blocks_ref.shape[0], blocks_ref.shape[1]
    part_rows = 4 * PLANE

    @pl.when(step == 0)
    def _():
        total[...] = jnp.zeros_like(total)
        centers[...] = center_ref[...].astype(jnp.float32)
        expos[...] = expo_ref[...].astype(jnp.float32)
        slopes[...] = slope_ref[...].astype(jnp.float32)

    def factors(block, which, slot):
        def spread(ref, index):
            return jnp.broadcast_to(ref[pl.ds(index, 1), :], (TE, width))

        return side_factors(
            [spread(centers, 6 * block + 2 * a + which) for a in range(3)],
            spread(expos, 2 * block + which),
            [spread(slopes, 6 * block + 2 * a + which) for a in range(3)],
            tables.at[slot],
        )

    ones = jnp.ones((16, width), jnp.bfloat16)
    transposed = (((1,), (1,)), ((), ()))

    for i in range(count):
        block = step * count + i
        column = columns[i]
        row, t, d = factors(block, 1, 2 * i)
        for x in range(TPB * TE):
            value = (t * row(x)[None]).reshape(PLANE, width)
            column[x * PLANE : (x + 1) * PLANE, :] = value.astype(jnp.bfloat16)
            t = t + d
        product = lax.dot_general(
            column[...], blocks_ref[i], transposed, preferred_element_type=jnp.float32
        )
        row, t, d = factors(block, 0, 2 * i + 1)
        for part in range(TPB * CELLS // part_rows):
            planes = []
            for x in range(4 * part, 4 * part + 4):
                value = (t * row(x)[None]).reshape(PLANE, width)
                value = value * product[x * PLANE : (x + 1) * PLANE, :]
                planes.append(value.astype(jnp.bfloat16))
                t = t + d
            scaled = jnp.concatenate(planes, axis=0)
            sums = lax.dot_general(ones, scaled, transposed, preferred_element_type=jnp.float32)
            k, q = divmod(part * part_rows, CELLS)
            where = row_of(dest_ref, tile_ref, block, k)
            total[pl.ds(where, 1), q : q + part_rows] += sums[0:1]

    @pl.when(step == pl.num_programs(0) - 1)
    def _():
        out_ref[...] = (2.0 * total[...]).astype(out_ref.dtype)


def tile_sums(blocks, center, expo, slope, dest, tiles, row_of, row_count, out_type):
    number, width = blocks.shape[0], blocks.shape[1]
    per_step = min(STEP_BLOCKS, number)

    def flat(values):
        return values.reshape(-1, width)

    def whole(values):
        return pl.BlockSpec(values.shape, lambda g: (0, 0))

    tables = (flat(jnp.swapaxes(center, 1, 2)), flat(expo), flat(jnp.swapaxes(slope, 1, 2)))
    scalars = pl.BlockSpec(memory_space=pltpu.SMEM)
    return pl.pallas_call(
        functools.partial(density_kernel, row_of=row_of),
        grid=(number // per_step,),
        in_specs=[
            scalars,
            scalars,
            pl.BlockSpec((per_step, width, width), lambda g: (g, 0, 0)),
            *[whole(values) for values in tables],
        ],
        out_specs=pl.BlockSpec((row_count, CELLS), lambda g: (0, 0)),
        out_shape=jax.ShapeDtypeStruct((row_count, CELLS), out_type),
        scratch_shapes=[
            pltpu.VMEM((row_count, CELLS), jnp.float32),
            *[pltpu.VMEM(values.shape, jnp.float32) for values in tables],
            pltpu.VMEM((2 * per_step, (TPB + 2) * TE, width), jnp.float32),
            *[pltpu.VMEM((TPB * CELLS, width), jnp.bfloat16)] * per_step,
        ],
        compiler_params=pltpu.CompilerParams(vmem_limit_bytes=60 << 20),
    )(dest.T, tiles.T, blocks, *tables)


def pick_rows(summed, order):
    match = order[:, None] == jnp.arange(summed.shape[0], dtype=jnp.int32)[None, :]
    return jnp.sum(jnp.where(match[:, :, None], summed[None], 0.0), axis=1)


def dense_plan(blocks, center, expo, slope, dest, tiles, order, dom_count, sub_count):
    quarter = TPD // sub_count
    held = dom_count * quarter

    def row_of(dest_ref, tile_ref, block, k):
        tile = tile_ref[k, block]
        return tile // quarter * held + dest_ref[0, block] * quarter + tile % quarter

    partial = tile_sums(
        blocks, center, expo, slope, dest, tiles, row_of, dom_count * sub_count * held, jnp.bfloat16
    )
    moved = lax.all_to_all(
        partial.reshape(dom_count * sub_count, held, CELLS), AXES, split_axis=0, concat_axis=0, tiled=True
    )
    return pick_rows(jnp.sum(moved.astype(jnp.float32), axis=0), order)


def routed_plan(blocks, center, expo, slope, dest, tiles, order, dom_count, sub_count):
    number = blocks.shape[0]
    capacity = max(2, 2 * number // dom_count)
    tile_count = dom_count * TPD
    quarter = TPD // sub_count

    def row_of(dest_ref, tile_ref, block, k):
        return TPB * block + k

    density = tile_sums(
        blocks, center, expo, slope, dest, tiles, row_of, TPB * number, jnp.float32
    )
    density = density.reshape(number, TPB, CELLS).astype(jnp.bfloat16)
    targets = dest[:, 0]
    one_hot = (targets[:, None] == jnp.arange(dom_count, dtype=jnp.int32)[None, :]).astype(jnp.int32)
    places = jnp.sum((jnp.cumsum(one_hot, axis=0) - one_hot) * one_hot, axis=1)

    def exchange(values, filler):
        holder = jnp.full((dom_count, capacity) + values.shape[1:], filler, values.dtype)
        holder = holder.at[targets, places].set(values)
        return lax.all_to_all(holder, "dom", split_axis=0, concat_axis=0, tiled=True)

    arrived = exchange(density, 0).reshape(-1, CELLS).astype(jnp.float32)
    tile_ids = exchange(tiles, tile_count).reshape(-1)
    partial = jnp.zeros((tile_count, CELLS), jnp.float32).at[tile_ids].add(arrived, mode="drop")
    moved = lax.all_to_all(
        partial.reshape(dom_count, TPD, CELLS), "dom", split_axis=0, concat_axis=0, tiled=True
    )
    summed = lax.psum_scatter(moved, "sub", scatter_dimension=1, tiled=True)
    return summed.reshape(dom_count * quarter, CELLS)[order]


def local(blocks, center, expo, slope, dest, tiles, slab_from):
    dom_count, sub_count = lax.axis_size("dom"), lax.axis_size("sub")
    all_rows = dom_count * dom_count * TPD
    plan = dense_plan if all_rows <= DENSE_ROWS else routed_plan
    return plan(blocks, center, expo, slope, dest, tiles, slab_from[0], dom_count, sub_count)


def solution(mesh):
    def placed(rank):
        return P(AXES, *([None] * (rank - 1)))

    return jax.shard_map(
        local,
        mesh=mesh,
        in_specs=tuple(placed(rank) for rank in (3, 4, 3, 4, 2, 2, 2)),
        out_specs=placed(2),
        check_vma=False,
    )
```

```python
import functools

import jax
import jax.numpy as jnp
from jax import lax
from jax.experimental import pallas as pl
from jax.experimental.pallas import tpu as pltpu
from jax.sharding import PartitionSpec as P

TE = 8
TPB = 2
TPD = 4
CELLS = TE**3
PLANE = TE * TE
AXES = ("dom", "sub")
STEP_BLOCKS = 32
LOG2_E = 1.4426950408889634
DENSE_ROWS = 1024


def side_factors(center, expo, slope, table):
    width = expo.shape[-1]
    steps = lax.broadcasted_iota(jnp.int32, (TE, width), 0).astype(jnp.float32)
    center_x = float(TPB) * center[0]
    rate = expo * (-LOG2_E)
    uy = steps - center[1]
    uz = steps - center[2]
    for k in range(TPB):
        ux = (steps + float(k * TE)) - center_x
        table[k * TE : (k + 1) * TE, :] = jnp.exp2(rate * (ux * ux))
    y_rows, slope_rows = TPB * TE, (TPB + 1) * TE
    table[y_rows : y_rows + TE, :] = jnp.exp2(rate * (uy * uy))
    table[slope_rows : slope_rows + TE, :] = (1.0 - slope[0] * center_x) + slope[1] * uy
    ez = jnp.exp2(rate * (uz * uz))
    z_part = slope[2] * uz

    def row(index):
        return jnp.broadcast_to(table[index : index + 1, :], (TE, width))

    yz = [row(y_rows + y) * ez for y in range(TE)]
    t = jnp.stack([yz[y] * (row(slope_rows + y) + z_part) for y in range(TE)])
    d = jnp.stack([value * slope[0] for value in yz])
    return row, t, d


def density_kernel(
    dest_ref,
    tile_ref,
    blocks_ref,
    center_ref,
    expo_ref,
    slope_ref,
    out_ref,
    total,
    centers,
    expos,
    slopes,
    tables,
    *,
    row_of,
):
    step = pl.program_id(0)
    count, width = blocks_ref.shape[0], blocks_ref.shape[1]
    part_rows = 4 * PLANE

    @pl.when(step == 0)
    def _():
        total[...] = jnp.zeros_like(total)
        centers[...] = center_ref[...].astype(jnp.float32)
        expos[...] = expo_ref[...].astype(jnp.float32)
        slopes[...] = slope_ref[...].astype(jnp.float32)

    def factors(block, which, slot):
        def spread(ref, index):
            return jnp.broadcast_to(ref[pl.ds(index, 1), :], (TE, width))

        return side_factors(
            [spread(centers, 6 * block + 2 * a + which) for a in range(3)],
            spread(expos, 2 * block + which),
            [spread(slopes, 6 * block + 2 * a + which) for a in range(3)],
            tables.at[slot],
        )

    ones = jnp.ones((16, width), jnp.bfloat16)
    transposed = (((1,), (1,)), ((), ()))

    for i in range(count):
        block = step * count + i
        row, t, d = factors(block, 1, 2 * i)
        planes = []
        for x in range(TPB * TE):
            value = (t * row(x)[None]).reshape(PLANE, width)
            planes.append(value.astype(jnp.bfloat16))
            t = t + d
        column = jnp.concatenate(planes, axis=0)
        product = lax.dot_general(
            column, blocks_ref[i], transposed, preferred_element_type=jnp.float32
        )
        row, t, d = factors(block, 0, 2 * i + 1)
        for part in range(TPB * CELLS // part_rows):
            planes = []
            for x in range(4 * part, 4 * part + 4):
                value = (t * row(x)[None]).reshape(PLANE, width)
                value = value * product[x * PLANE : (x + 1) * PLANE, :]
                planes.append(value.astype(jnp.bfloat16))
                t = t + d
            scaled = jnp.concatenate(planes, axis=0)
            sums = lax.dot_general(ones, scaled, transposed, preferred_element_type=jnp.float32)
            k, q = divmod(part * part_rows, CELLS)
            where = row_of(dest_ref, tile_ref, block, k)
            total[pl.ds(where, 1), q : q + part_rows] += sums[0:1]

    @pl.when(step == pl.num_programs(0) - 1)
    def _():
        out_ref[...] = (2.0 * total[...]).astype(out_ref.dtype)


def tile_sums(blocks, center, expo, slope, dest, tiles, row_of, row_count, out_type):
    number, width = blocks.shape[0], blocks.shape[1]
    per_step = min(STEP_BLOCKS, number)

    def flat(values):
        return values.reshape(-1, width)

    def whole(values):
        return pl.BlockSpec(values.shape, lambda g: (0, 0))

    tables = (flat(jnp.swapaxes(center, 1, 2)), flat(expo), flat(jnp.swapaxes(slope, 1, 2)))
    scalars = pl.BlockSpec(memory_space=pltpu.SMEM)
    return pl.pallas_call(
        functools.partial(density_kernel, row_of=row_of),
        grid=(number // per_step,),
        in_specs=[
            scalars,
            scalars,
            pl.BlockSpec((per_step, width, width), lambda g: (g, 0, 0)),
            *[whole(values) for values in tables],
        ],
        out_specs=pl.BlockSpec((row_count, CELLS), lambda g: (0, 0)),
        out_shape=jax.ShapeDtypeStruct((row_count, CELLS), out_type),
        scratch_shapes=[
            pltpu.VMEM((row_count, CELLS), jnp.float32),
            *[pltpu.VMEM(values.shape, jnp.float32) for values in tables],
            pltpu.VMEM((2 * per_step, (TPB + 2) * TE, width), jnp.float32),
        ],
        compiler_params=pltpu.CompilerParams(vmem_limit_bytes=60 << 20),
    )(dest.T, tiles.T, blocks, *tables)


def pick_rows(summed, order):
    match = order[:, None] == jnp.arange(summed.shape[0], dtype=jnp.int32)[None, :]
    return jnp.sum(jnp.where(match[:, :, None], summed[None], 0.0), axis=1)


def dense_plan(blocks, center, expo, slope, dest, tiles, order, dom_count, sub_count):
    quarter = TPD // sub_count
    held = dom_count * quarter

    def row_of(dest_ref, tile_ref, block, k):
        tile = tile_ref[k, block]
        return tile // quarter * held + dest_ref[0, block] * quarter + tile % quarter

    partial = tile_sums(
        blocks, center, expo, slope, dest, tiles, row_of, dom_count * sub_count * held, jnp.bfloat16
    )
    moved = lax.all_to_all(
        partial.reshape(dom_count * sub_count, held, CELLS), AXES, split_axis=0, concat_axis=0, tiled=True
    )
    return pick_rows(jnp.sum(moved.astype(jnp.float32), axis=0), order)


def routed_plan(blocks, center, expo, slope, dest, tiles, order, dom_count, sub_count):
    number = blocks.shape[0]
    capacity = max(2, 2 * number // dom_count)
    tile_count = dom_count * TPD
    quarter = TPD // sub_count

    def row_of(dest_ref, tile_ref, block, k):
        return TPB * block + k

    density = tile_sums(
        blocks, center, expo, slope, dest, tiles, row_of, TPB * number, jnp.float32
    )
    density = density.reshape(number, TPB, CELLS).astype(jnp.bfloat16)
    targets = dest[:, 0]
    one_hot = (targets[:, None] == jnp.arange(dom_count, dtype=jnp.int32)[None, :]).astype(jnp.int32)
    places = jnp.sum((jnp.cumsum(one_hot, axis=0) - one_hot) * one_hot, axis=1)

    def exchange(values, filler):
        holder = jnp.full((dom_count, capacity) + values.shape[1:], filler, values.dtype)
        holder = holder.at[targets, places].set(values)
        return lax.all_to_all(holder, "dom", split_axis=0, concat_axis=0, tiled=True)

    arrived = exchange(density, 0).reshape(-1, CELLS).astype(jnp.float32)
    tile_ids = exchange(tiles, tile_count).reshape(-1)
    partial = jnp.zeros((tile_count, CELLS), jnp.float32).at[tile_ids].add(arrived, mode="drop")
    moved = lax.all_to_all(
        partial.reshape(dom_count, TPD, CELLS), "dom", split_axis=0, concat_axis=0, tiled=True
    )
    summed = lax.psum_scatter(moved, "sub", scatter_dimension=1, tiled=True)
    return summed.reshape(dom_count * quarter, CELLS)[order]


def local(blocks, center, expo, slope, dest, tiles, slab_from):
    dom_count, sub_count = lax.axis_size("dom"), lax.axis_size("sub")
    all_rows = dom_count * dom_count * TPD
    plan = dense_plan if all_rows <= DENSE_ROWS else routed_plan
    return plan(blocks, center, expo, slope, dest, tiles, slab_from[0], dom_count, sub_count)


def solution(mesh):
    def placed(rank):
        return P(AXES, *([None] * (rank - 1)))

    return jax.shard_map(
        local,
        mesh=mesh,
        in_specs=tuple(placed(rank) for rank in (3, 4, 3, 4, 2, 2, 2)),
        out_specs=placed(2),
        check_vma=False,
    )
```
